32 devices in a mesh: py: 8 (over y, x, core), px: 4 (over z).
Axes of the slice: x: 2, y: 2, z: 4, core: 2. Of those that a mesh axis runs over, the one named last changes fastest.
Arguments:
- frames: float32 [32, 512, 512], P(('px', 'py')), may hold values from -6 to 6
- shifts: int32 [32, 2], P(('px', 'py')), may hold values from -8 to 8
- start_basis: float32 [32, 16], replicated, may hold values from -6 to 6
Outputs:
- spatial_components: float32 [16, 512, 512], P(None, 'py', 'px')
- temporal_components: float32 [8, 8, 32, 16], P('py', 'px')
- background: float32 [512, 512], P('py', 'px')
The draws below stay inside these ranges and needn't reach their ends.
All inputs are finite; a program needn't handle non-finite values.
Results may differ from the reference program's by a relative error of at most 0.0003.
Values sent between devices are 32-bit elements; how exact they have to be, the bound alone decides.
A program may use at most 128 MiB of HBM per device.

```python
import jax
import jax.numpy as jnp
from jax import lax

PATCH = 64
MARGIN = 8
RANK = 16
ITERS = 6
SHIFT = 8
FRAMES = 32
HEIGHT = 512
WIDTH = 512


def with_ends(entries, own_key, least, high):
    shape = entries.shape
    place = [jax.random.randint(jax.random.fold_in(own_key, axis), (), 0, shape[axis]) for axis in range(len(shape))]
    entries = entries.at[tuple(place)].set(least)
    longest = shape.index(max(shape))
    place[longest] = (place[longest] + 1) % shape[longest]
    return entries.at[tuple(place)].set(high)


def block_scale(stream_key, extent, pieces, least, high):
    gain, own = 1.0, jax.random.fold_in(stream_key, 6)
    for position, parts in pieces:
        steps = jnp.exp(jax.random.uniform(jax.random.fold_in(own, position), (parts,), jnp.float32, least / len(pieces), high / len(pieces)))
        gain = gain * jnp.repeat(steps, extent[position] // parts).reshape([-1 if axis == position else 1 for axis in range(len(extent))])
    return gain


def normal_values(own_key, shape, spread, most, shards=(), held_as=jnp.bfloat16):
    values = jax.random.normal(own_key, shape, jnp.float32) * spread
    if len(shards) > 0:
        values = block_scale(own_key, shape, shards, -0.22, 0.18) * values
    return jnp.clip(values, min=-most, max=most).astype(held_as)


def setup_inputs(seed: int = 0) -> dict:
    arg_keys = jax.random.split(jax.random.key(seed), 4)
    return {
        "frames": normal_values(arg_keys[0], (FRAMES, HEIGHT, WIDTH), 1.0, 6.0, ((0, 32),), jnp.float32),
        "shifts": with_ends(jax.random.randint(arg_keys[1], (FRAMES, 2), -SHIFT, SHIFT + 1), jax.random.fold_in(arg_keys[1], 1), -SHIFT, SHIFT).astype(jnp.int32),
        "start_basis": normal_values(arg_keys[2], (FRAMES, RANK), 1.0, 6.0, (), jnp.float32),
    }


SHRINK = 0.5
EPSILON = 1e-06
HIGH = lax.Precision.HIGHEST

def orthonormal(matrix):
    count = matrix.shape[-1]
    ident = jnp.eye(count, dtype=matrix.dtype)
    result = matrix
    for sweep in range(2):
        gram = jnp.einsum('...tr,...ts->...rs', result, result, precision=HIGH) + EPSILON * ident
        lower = jnp.linalg.cholesky(gram)
        result = lax.linalg.triangular_solve(lower, result, left_side=False, lower=True, transpose_a=True)
    return result

def spatial_factor(basis, movie, pixel_mean):
    projected = jnp.einsum('...tr,...tk->...rk', basis, movie, precision=HIGH)
    projected = projected - lax.optimization_barrier(jnp.sum(basis, axis=-2))[..., :, None] * pixel_mean[..., None, :]
    level = SHRINK * jnp.sqrt(lax.optimization_barrier(jnp.mean(projected * projected, axis=-1, keepdims=True)) + EPSILON)
    return projected - jnp.clip(projected, -level, level)

def temporal_update(factor, movie, pixel_mean):
    product = jnp.einsum('...tk,...rk->...tr', movie, factor, precision=HIGH)
    offset = jnp.einsum('...k,...rk->...r', pixel_mean, factor, precision=HIGH)
    return orthonormal(product - offset[..., None, :])

def decompose(movie, start):
    pixel_mean = lax.optimization_barrier(jnp.mean(movie, axis=-2))
    basis = start
    for step in range(ITERS):
        factor = spatial_factor(basis, movie, pixel_mean)
        basis = temporal_update(factor, movie, pixel_mean)
    factor = spatial_factor(basis, movie, pixel_mean)
    return (factor, basis, pixel_mean)

def reference(frames, shifts, start_basis):
    edge = PATCH + 2 * MARGIN
    reach = SHIFT + MARGIN
    patch_rows = HEIGHT // PATCH
    patch_cols = WIDTH // PATCH
    padded = jnp.pad(frames, ((0, 0), (reach, reach), (reach, reach)))
    start = orthonormal(start_basis)
    offsets = jnp.arange(edge, dtype=jnp.int32)

    def one_patch(patch_id):
        top = patch_id // patch_cols * PATCH - MARGIN
        left = patch_id % patch_cols * PATCH - MARGIN

        def cut(frame, offset):
            row0 = (top - offset[0] + reach).astype(jnp.int32)
            col0 = (left - offset[1] + reach).astype(jnp.int32)
            return lax.dynamic_slice(frame, (row0, col0), (edge, edge))
        window = jax.vmap(cut)(padded, shifts)
        rows_in = (top + offsets >= 0) & (top + offsets < HEIGHT)
        cols_in = (left + offsets >= 0) & (left + offsets < WIDTH)
        inside = (rows_in[:, None] & cols_in[None, :]).astype(jnp.float32)
        movie = (window * inside[None]).reshape(FRAMES, edge * edge)
        factor, basis, pixel_mean = decompose(movie, start)
        factor = factor.reshape(RANK, edge, edge)[:, MARGIN:MARGIN + PATCH, MARGIN:MARGIN + PATCH]
        pixel_mean = pixel_mean.reshape(edge, edge)[MARGIN:MARGIN + PATCH, MARGIN:MARGIN + PATCH]
        return (factor, basis, pixel_mean)
    patch_ids = jnp.arange(patch_rows * patch_cols, dtype=jnp.int32)
    factors, bases, means = lax.map(one_patch, patch_ids)
    spatial = factors.reshape(patch_rows, patch_cols, RANK, PATCH, PATCH).transpose(2, 0, 3, 1, 4).reshape(RANK, HEIGHT, WIDTH)
    temporal = bases.reshape(patch_rows, patch_cols, FRAMES, RANK) * jnp.sqrt(jnp.float32(FRAMES))
    background = means.reshape(patch_rows, patch_cols, PATCH, PATCH).transpose(0, 2, 1, 3).reshape(HEIGHT, WIDTH)
    return (spatial, temporal, background)
```

```python
import functools

import jax
import jax.numpy as jnp
from jax import lax
from jax.experimental import pallas as pl
from jax.experimental.pallas import tpu as pltpu
from jax.sharding import PartitionSpec as P

PATCH = 64
MARGIN = 8
RANK = 16
ITERS = 6
SHIFT = 8
EDGE = PATCH + 2 * MARGIN
COLS = 2 * PATCH
CORE = EDGE * COLS
SIDE = EDGE * 2 * MARGIN
PIXELS = CORE + SIDE
CHUNK = SIDE
CHUNKS = PIXELS // CHUNK

SHRINK = 0.5
EPSILON = 1e-06
HIGH = lax.Precision.HIGHEST
NT = (((1,), (1,)), ((), ()))


def halves(value):
    high = value.astype(jnp.bfloat16)
    low = (value - high.astype(jnp.float32)).astype(jnp.bfloat16)
    return high, low


def orthonormal_rows(rows):
    rank = lax.broadcasted_iota(jnp.int32, (RANK, 1), 0)
    eye = (
        lax.broadcasted_iota(jnp.int32, (RANK, RANK), 0)
        == lax.broadcasted_iota(jnp.int32, (RANK, RANK), 1)
    )
    for sweep in range(2):
        grams = [
            lax.dot_general(z, z, NT, precision=HIGH, preferred_element_type=jnp.float32)
            + jnp.where(eye, EPSILON, 0.0)
            for z in rows
        ]
        for j in range(RANK - 1):
            for p in range(len(rows)):
                gram, z = grams[p], rows[p]
                ratio = gram[:, j : j + 1] * (1.0 / gram[j : j + 1, j : j + 1])
                ratio = jnp.where(rank > j, ratio, 0.0)
                grams[p] = gram - ratio * gram[j : j + 1, :]
                rows[p] = z - ratio * z[j : j + 1, :]
        for p in range(len(rows)):
            pivot = jnp.sum(jnp.where(eye, grams[p], 0.0), axis=1, keepdims=True)
            rows[p] = rows[p] * lax.rsqrt(pivot)
    return rows


def decompose_kernel(movie_ref, start_ref, spatial_ref, basis_ref, mean_ref, parts, proj):
    frames = movie_ref.shape[0]
    for c in range(CHUNKS):
        at = pl.ds(c * CHUNK, CHUNK)
        raw = movie_ref[:, at]
        mean = jnp.sum(raw, axis=0, keepdims=True) * (1.0 / frames)
        mean_ref[:, at] = mean
        high, low = halves(raw - mean)
        for part, value in enumerate((high, low, high, low)):
            parts[part * frames : (part + 1) * frames, at] = value

    lane = lax.broadcasted_iota(jnp.int32, (2 * RANK, CHUNK), 1)
    patch = lax.broadcasted_iota(jnp.int32, (2 * RANK, CHUNK), 0) // RANK
    from_left = lane % COLS - patch * (PATCH - MARGIN)
    core_mask = (from_left >= 0) & (from_left < PATCH + MARGIN)
    side_mask = lane % (2 * MARGIN) // MARGIN == patch

    def project(basis):
        high = basis.astype(jnp.bfloat16).astype(jnp.float32)
        low = basis - high
        left = jnp.concatenate([high, high, low, low], axis=1).astype(jnp.bfloat16)
        total = jnp.zeros((2 * RANK, 128), jnp.float32)
        for c in range(CHUNKS):
            at = pl.ds(c * CHUNK, CHUNK)
            value = jnp.dot(left, parts[:, at], preferred_element_type=jnp.float32)
            value = jnp.where(core_mask if c < CHUNKS - 1 else side_mask, value, 0.0)
            proj[:, at] = value
            square = value * value
            for t in range(CHUNK // 128):
                total = total + square[:, t * 128 : (t + 1) * 128]
        power = jnp.sum(total, axis=1, keepdims=True) * (1.0 / (EDGE * EDGE))
        return SHRINK * jnp.sqrt(power + EPSILON)

    def shrunk(level, at):
        value = proj[:, at]
        return value - jnp.clip(value, -level, level)

    def step(_, basis):
        level = project(basis)
        total = jnp.zeros((4 * RANK, 2 * frames), jnp.float32)
        for c in range(CHUNKS):
            at = pl.ds(c * CHUNK, CHUNK)
            factor = jnp.concatenate(halves(shrunk(level, at)), axis=0)
            total = total + lax.dot_general(
                factor, parts[: 2 * frames, at], NT, preferred_element_type=jnp.float32
            )
        total = total[: 2 * RANK] + total[2 * RANK :]
        total = total[:, :frames] + total[:, frames:]
        return jnp.concatenate(orthonormal_rows([total[:RANK], total[RANK:]]), axis=0)

    start = orthonormal_rows([start_ref[...]])[0]
    basis = lax.fori_loop(0, ITERS, step, jnp.concatenate([start, start], axis=0))
    basis_ref[...] = basis
    level = project(basis)
    left_half = lax.broadcasted_iota(jnp.int32, (RANK, COLS), 1) < PATCH
    for row in range(PATCH):
        factor = shrunk(level, pl.ds((row + MARGIN) * COLS, COLS))
        spatial_ref[:, row * COLS : (row + 1) * COLS] = jnp.where(
            left_half, factor[:RANK], factor[RANK:]
        )


def decompose(movie, start):
    frames = movie.shape[0]
    vmem = pl.BlockSpec(memory_space=pltpu.VMEM)
    return pl.pallas_call(
        decompose_kernel,
        out_shape=(
            jax.ShapeDtypeStruct((RANK, PATCH * COLS), jnp.float32),
            jax.ShapeDtypeStruct((2 * RANK, frames), jnp.float32),
            jax.ShapeDtypeStruct((1, PIXELS), jnp.float32),
        ),
        in_specs=[vmem, vmem],
        out_specs=(vmem, vmem, vmem),
        scratch_shapes=[
            pltpu.VMEM((4 * frames, PIXELS), jnp.bfloat16),
            pltpu.VMEM((2 * RANK, PIXELS), jnp.float32),
        ],
        compiler_params=pltpu.CompilerParams(vmem_limit_bytes=48 * 1024 * 1024),
        name="decompose",
    )(movie, start)


def place_frame(frame, offset):
    height, width = frame.shape
    padded = jnp.pad(frame, SHIFT + MARGIN)
    size = (height + 2 * MARGIN, width + 2 * MARGIN)
    moved = lax.dynamic_slice(padded, (SHIFT - offset[0], SHIFT - offset[1]), size)
    row = lax.broadcasted_iota(jnp.int32, size, 0)
    col = lax.broadcasted_iota(jnp.int32, size, 1)
    inside = (row >= MARGIN) & (row < MARGIN + height) & (col >= MARGIN) & (col < MARGIN + width)
    return jnp.where(inside, moved, 0.0)


def blocks_of(frame, n_rows, n_cols):
    tops = [r * PATCH for r in range(n_rows)]
    middle = frame[:, MARGIN : MARGIN + n_cols * COLS]
    core = jnp.stack([middle[t : t + EDGE] for t in tops])
    core = core.reshape(n_rows, EDGE, n_cols, COLS).transpose(2, 0, 1, 3)
    sides = []
    for c in range(n_cols):
        left = frame[:, c * COLS : c * COLS + MARGIN]
        start = MARGIN + (c + 1) * COLS
        both = jnp.concatenate([left, frame[:, start : start + MARGIN]], axis=1)
        sides.append(jnp.stack([both[t : t + EDGE] for t in tops]))
    sides = jnp.stack(sides).reshape(n_cols, n_rows, SIDE // COLS, COLS)
    return jnp.concatenate([core, sides], axis=2)


def on_device(frames, shifts, start_basis):
    n_rows = lax.axis_size("py")
    n_cols = lax.axis_size("px")
    assert frames.shape[1:] == (n_rows * PATCH, n_cols * COLS)
    placed = jax.vmap(place_frame)(frames, shifts)
    blocks = jax.vmap(functools.partial(blocks_of, n_rows=n_rows, n_cols=n_cols))(placed)
    blocks = blocks.reshape(frames.shape[0], n_rows * n_cols, PIXELS // COLS, COLS)
    arrived = lax.all_to_all(blocks, ("px", "py"), split_axis=1, concat_axis=0, tiled=True)
    total_frames = arrived.shape[0]
    movie = arrived.reshape(total_frames, PIXELS)
    spatial, basis, mean = decompose(movie, start_basis.T)
    spatial = spatial.reshape(RANK, PATCH, COLS)
    temporal = basis.reshape(1, 2, RANK, total_frames).transpose(0, 1, 3, 2) * jnp.sqrt(
        jnp.float32(total_frames)
    )
    background = mean[0, MARGIN * COLS : (MARGIN + PATCH) * COLS].reshape(PATCH, COLS)
    return (spatial, temporal, background)


def solution(mesh):
    placed = (P(("px", "py"), None, None), P(("px", "py"), None), P())
    return jax.shard_map(
        on_device,
        mesh=mesh,
        in_specs=placed,
        out_specs=(P(None, "py", "px"), P("py", "px", None, None), P("py", "px")),
        check_vma=False,
    )
```

```python
import jax
import jax.numpy as jnp
from jax import lax
from jax.experimental import pallas as pl
from jax.experimental.pallas import tpu as pltpu
from jax.sharding import PartitionSpec as P

PATCH = 64
MARGIN = 8
RANK = 16
ITERS = 6
SHIFT = 8
EDGE = PATCH + 2 * MARGIN
COLS = 2 * PATCH
CORE = EDGE * COLS
SIDE = EDGE * 2 * MARGIN
PIXELS = CORE + SIDE
CHUNK = SIDE
CHUNKS = PIXELS // CHUNK

SHRINK = 0.5
EPSILON = 1e-06
HIGH = lax.Precision.HIGHEST
NT = (((1,), (1,)), ((), ()))


def halves(value):
    high = value.astype(jnp.bfloat16)
    low = (value - high.astype(jnp.float32)).astype(jnp.bfloat16)
    return high, low


def orthonormal_rows(rows):
    rank = lax.broadcasted_iota(jnp.int32, (RANK, 1), 0)
    eye = (
        lax.broadcasted_iota(jnp.int32, (RANK, RANK), 0)
        == lax.broadcasted_iota(jnp.int32, (RANK, RANK), 1)
    )
    before = (
        lax.broadcasted_iota(jnp.int32, (RANK, RANK), 0)
        == lax.broadcasted_iota(jnp.int32, (RANK, RANK), 1) + 1
    )
    for sweep in range(2):
        grams = [
            lax.dot_general(z, z, NT, precision=HIGH, preferred_element_type=jnp.float32)
            + jnp.where(eye, EPSILON, 0.0)
            for z in rows
        ]
        for j in range(0, RANK - 2, 2):
            for p in range(len(rows)):
                gram, z = grams[p], rows[p]
                a = gram[j : j + 1, j : j + 1]
                b = gram[j : j + 1, j + 1 : j + 2]
                c = gram[j + 1 : j + 2, j + 1 : j + 2]
                inverse = 1.0 / (c - b * (b / a))
                below = rank > j + 1
                ratio0 = jnp.where(below, gram[:, j : j + 1], 0.0)
                ratio1 = jnp.where(below, gram[:, j + 1 : j + 2], 0.0)
                ratio1 = (ratio1 - ratio0 * (b / a)) * inverse
                ratio0 = ratio0 / a - ratio1 * (b / a)
                grams[p] = gram - ratio0 * gram[j : j + 1] - ratio1 * gram[j + 1 : j + 2]
                rows[p] = z - ratio0 * z[j : j + 1] - ratio1 * z[j + 1 : j + 2]
        for p in range(len(rows)):
            gram, z = grams[p], rows[p]
            diagonal = jnp.sum(jnp.where(eye, gram, 0.0), axis=1, keepdims=True)
            below = jnp.sum(jnp.where(before, gram, 0.0), axis=1, keepdims=True)
            ratio = jnp.where(rank % 2 == 1, below / pltpu.roll(diagonal, 1, 0), 0.0)
            pivot = diagonal - ratio * below
            rows[p] = (z - ratio * pltpu.roll(z, 1, 0)) * lax.rsqrt(pivot)
    return rows


def decompose_kernel(movie_ref, start_ref, spatial_ref, basis_ref, mean_ref, parts, proj):
    frames = movie_ref.shape[0]
    for c in range(CHUNKS):
        at = pl.ds(c * CHUNK, CHUNK)
        first_row = c * (CHUNK // COLS)
        raw = jnp.concatenate(
            [movie_ref[:, first_row + i, :] for i in range(CHUNK // COLS)], axis=1
        )
        mean = jnp.sum(raw, axis=0, keepdims=True) * (1.0 / frames)
        mean_ref[:, at] = mean
        high, low = halves(raw - mean)
        for part, value in enumerate((high, low, high, low)):
            parts[part * frames : (part + 1) * frames, at] = value

    lane = lax.broadcasted_iota(jnp.int32, (2 * RANK, CHUNK), 1)
    patch = lax.broadcasted_iota(jnp.int32, (2 * RANK, CHUNK), 0) // RANK
    from_left = lane % COLS - patch * (PATCH - MARGIN)
    core_mask = (from_left >= 0) & (from_left < PATCH + MARGIN)
    side_mask = lane % (2 * MARGIN) // MARGIN == patch

    def project(basis):
        high = basis.astype(jnp.bfloat16).astype(jnp.float32)
        low = basis - high
        left = jnp.concatenate([high, high, low, low], axis=1).astype(jnp.bfloat16)
        total = jnp.zeros((2 * RANK, 128), jnp.float32)
        for c in range(CHUNKS):
            at = pl.ds(c * CHUNK, CHUNK)
            value = jnp.dot(left, parts[:, at], preferred_element_type=jnp.float32)
            value = jnp.where(core_mask if c < CHUNKS - 1 else side_mask, value, 0.0)
            proj[:, at] = value
            square = value * value
            for t in range(CHUNK // 128):
                total = total + square[:, t * 128 : (t + 1) * 128]
        power = jnp.sum(total, axis=1, keepdims=True) * (1.0 / (EDGE * EDGE))
        return SHRINK * jnp.sqrt(power + EPSILON)

    def shrunk(level, at):
        value = proj[:, at]
        return value - jnp.clip(value, -level, level)

    def step(_, basis):
        level = project(basis)
        total = jnp.zeros((4 * RANK, 2 * frames), jnp.float32)
        for c in range(CHUNKS):
            at = pl.ds(c * CHUNK, CHUNK)
            factor = jnp.concatenate(halves(shrunk(level, at)), axis=0)
            total = total + lax.dot_general(
                factor, parts[: 2 * frames, at], NT, preferred_element_type=jnp.float32
            )
        total = total[: 2 * RANK] + total[2 * RANK :]
        total = total[:, :frames] + total[:, frames:]
        return jnp.concatenate(orthonormal_rows([total[:RANK], total[RANK:]]), axis=0)

    start = orthonormal_rows([start_ref[...]])[0]
    basis = lax.fori_loop(0, ITERS, step, jnp.concatenate([start, start], axis=0))
    basis_ref[...] = basis
    level = project(basis)
    left_half = lax.broadcasted_iota(jnp.int32, (RANK, COLS), 1) < PATCH
    for row in range(PATCH):
        factor = shrunk(level, pl.ds((row + MARGIN) * COLS, COLS))
        spatial_ref[:, row * COLS : (row + 1) * COLS] = jnp.where(
            left_half, factor[:RANK], factor[RANK:]
        )


def decompose(movie, start):
    frames = movie.shape[0]
    vmem = pl.BlockSpec(memory_space=pltpu.VMEM)
    return pl.pallas_call(
        decompose_kernel,
        out_shape=(
            jax.ShapeDtypeStruct((RANK, PATCH * COLS), jnp.float32),
            jax.ShapeDtypeStruct((2 * RANK, frames), jnp.float32),
            jax.ShapeDtypeStruct((1, PIXELS), jnp.float32),
        ),
        in_specs=[vmem, vmem],
        out_specs=(vmem, vmem, vmem),
        scratch_shapes=[
            pltpu.VMEM((4 * frames, PIXELS), jnp.bfloat16),
            pltpu.VMEM((2 * RANK, PIXELS), jnp.float32),
        ],
        compiler_params=pltpu.CompilerParams(vmem_limit_bytes=48 * 1024 * 1024),
        name="decompose",
    )(movie, start)


def place_kernel(shift_ref, frame_ref, out_ref, padded):
    height, width = frame_ref.shape
    n_cols, n_rows = out_ref.shape[:2]
    edge = SHIFT + MARGIN
    down, right = shift_ref[0], shift_ref[1]
    padded[:edge] = jnp.zeros((edge, width), jnp.float32)
    padded[edge : edge + height] = frame_ref[...]
    padded[edge + height :] = jnp.zeros((padded.shape[0] - edge - height, width), jnp.float32)
    row = lax.broadcasted_iota(jnp.int32, (EDGE, width), 0)
    col = lax.broadcasted_iota(jnp.int32, (EDGE, width), 1)
    from_col = col - right
    col_inside = (from_col >= 0) & (from_col < width)
    lane = lax.broadcasted_iota(jnp.int32, (EDGE, COLS), 1)
    row_in_tile = lax.broadcasted_iota(jnp.int32, (8, COLS), 0)
    turn = jnp.where(right < 0, right + width, right)
    ahead = SHIFT - down
    skip = ahead // 8 * 8
    lift = (EDGE + 8 - ahead % 8) % (EDGE + 8)
    nothing = jnp.zeros((EDGE, COLS), jnp.float32)
    for r in range(n_rows):
        top = r * PATCH - MARGIN
        block = padded[pl.ds(pl.multiple_of(r * PATCH + skip, 8), EDGE + 8), :]
        block = pltpu.roll(block, lift, 0)[:EDGE]
        inside = col_inside & (row + top >= 0) & (row + top < height)
        block = jnp.where(inside, pltpu.roll(block, turn, 1), 0.0)
        tiles = [block[:, c * COLS : (c + 1) * COLS] for c in range(n_cols)]
        for c in range(n_cols):
            out_ref[c, r, :EDGE, :] = tiles[c]
            left = tiles[c - 1] if c > 0 else nothing
            after = tiles[c + 1] if c + 1 < n_cols else nothing
            sides = jnp.where(lane >= COLS - MARGIN, left, jnp.where(lane < MARGIN, after, 0.0))
            group = [
                pltpu.roll(sides[8 * g : 8 * g + 8], (MARGIN + 2 * MARGIN * g) % COLS, 1)
                for g in range(EDGE // 8)
            ]
            out_ref[c, r, EDGE : EDGE + 8, :] = sum(group[1:8], group[0])
            rest = group[8] + group[9]
            spread = jnp.where(row_in_tile % 4 == 0, rest, 0.0)
            for q in range(1, 4):
                spread += jnp.where(row_in_tile % 4 == q, pltpu.roll(rest, 32 * q, 1), 0.0)
            for half in range(2):
                part = jnp.where(row_in_tile // 4 == half, spread, 0.0)
                out_ref[c, r, EDGE + 8 + half : EDGE + 9 + half, :] = jnp.sum(
                    part, axis=0, keepdims=True
                )


def place(frame, shift, n_rows, n_cols):
    height, width = frame.shape
    vmem = pl.BlockSpec(memory_space=pltpu.VMEM)
    return pl.pallas_call(
        place_kernel,
        out_shape=jax.ShapeDtypeStruct((n_cols, n_rows, PIXELS // COLS, COLS), jnp.float32),
        in_specs=[pl.BlockSpec(memory_space=pltpu.SMEM), vmem],
        out_specs=vmem,
        scratch_shapes=[pltpu.VMEM((height + 2 * (SHIFT + MARGIN) + 8, width), jnp.float32)],
        compiler_params=pltpu.CompilerParams(vmem_limit_bytes=48 * 1024 * 1024),
        name="place",
    )(shift, frame)


def on_device(frames, shifts, start_basis):
    n_rows = lax.axis_size("py")
    n_cols = lax.axis_size("px")
    assert frames.shape[1:] == (n_rows * PATCH, n_cols * COLS)
    blocks = jnp.stack(
        [place(frames[f], shifts[f], n_rows, n_cols) for f in range(frames.shape[0])]
    )
    blocks = blocks.reshape(frames.shape[0], n_rows * n_cols, PIXELS // COLS, COLS)
    arrived = lax.all_to_all(blocks, ("px", "py"), split_axis=1, concat_axis=0, tiled=True)
    arrived = arrived.reshape(-1, PIXELS // COLS, COLS)
    total_frames = arrived.shape[0]
    spatial, basis, mean = decompose(arrived, start_basis.T)
    spatial = spatial.reshape(RANK, PATCH, COLS)
    temporal = basis.reshape(1, 2, RANK, total_frames).transpose(0, 1, 3, 2) * jnp.sqrt(
        jnp.float32(total_frames)
    )
    background = mean[0, MARGIN * COLS : (MARGIN + PATCH) * COLS].reshape(PATCH, COLS)
    return (spatial, temporal, background)


def solution(mesh):
    placed = (P(("px", "py"), None, None), P(("px", "py"), None), P())
    return jax.shard_map(
        on_device,
        mesh=mesh,
        in_specs=placed,
        out_specs=(P(None, "py", "px"), P("py", "px", None, None), P("py", "px")),
        check_vma=False,
    )
```

```python
import jax
import jax.numpy as jnp
from jax import lax
from jax.experimental import pallas as pl
from jax.experimental.pallas import tpu as pltpu
from jax.sharding import PartitionSpec as P

PATCH = 64
MARGIN = 8
RANK = 16
ITERS = 6
SHIFT = 8
EDGE = PATCH + 2 * MARGIN
COLS = 2 * PATCH
CORE = EDGE * COLS
SIDE = EDGE * 2 * MARGIN
PIXELS = CORE + SIDE
CHUNK = SIDE
CHUNKS = PIXELS // CHUNK

SHRINK = 0.5
EPSILON = 1e-06
HIGH = lax.Precision.HIGHEST
NT = (((1,), (1,)), ((), ()))


def halves(value):
    high = value.astype(jnp.bfloat16)
    low = (value - high.astype(jnp.float32)).astype(jnp.bfloat16)
    return high, low


def orthonormal_rows(rows):
    rank = lax.broadcasted_iota(jnp.int32, (RANK, 1), 0)
    eye = (
        lax.broadcasted_iota(jnp.int32, (RANK, RANK), 0)
        == lax.broadcasted_iota(jnp.int32, (RANK, RANK), 1)
    )
    for sweep in range(2):
        grams = [
            lax.dot_general(z, z, NT, precision=HIGH, preferred_element_type=jnp.float32)
            + jnp.where(eye, EPSILON, 0.0)
            for z in rows
        ]
        for j in range(RANK - 1):
            for p in range(len(rows)):
                gram, z = grams[p], rows[p]
                ratio = gram[:, j : j + 1] * (1.0 / gram[j : j + 1, j : j + 1])
                ratio = jnp.where(rank > j, ratio, 0.0)
                grams[p] = gram - ratio * gram[j : j + 1, :]
                rows[p] = z - ratio * z[j : j + 1, :]
        for p in range(len(rows)):
            pivot = jnp.sum(jnp.where(eye, grams[p], 0.0), axis=1, keepdims=True)
            rows[p] = rows[p] * lax.rsqrt(pivot)
    return rows


def decompose_kernel(movie_ref, start_ref, spatial_ref, basis_ref, mean_ref, parts, proj):
    frames = movie_ref.shape[0]
    for c in range(CHUNKS):
        at = pl.ds(c * CHUNK, CHUNK)
        first_row = c * (CHUNK // COLS)
        raw = jnp.concatenate(
            [movie_ref[:, first_row + i, :] for i in range(CHUNK // COLS)], axis=1
        )
        mean = jnp.sum(raw, axis=0, keepdims=True) * (1.0 / frames)
        mean_ref[:, at] = mean
        high, low = halves(raw - mean)
        for part, value in enumerate((high, low, high, low)):
            parts[part * frames : (part + 1) * frames, at] = value

    lane = lax.broadcasted_iota(jnp.int32, (2 * RANK, CHUNK), 1)
    patch = lax.broadcasted_iota(jnp.int32, (2 * RANK, CHUNK), 0) // RANK
    from_left = lane % COLS - patch * (PATCH - MARGIN)
    core_mask = (from_left >= 0) & (from_left < PATCH + MARGIN)
    side_mask = lane % (2 * MARGIN) // MARGIN == patch

    def project(basis):
        high = basis.astype(jnp.bfloat16).astype(jnp.float32)
        low = basis - high
        left = jnp.concatenate([high, high, low, low], axis=1).astype(jnp.bfloat16)
        total = jnp.zeros((2 * RANK, 128), jnp.float32)
        for c in range(CHUNKS):
            at = pl.ds(c * CHUNK, CHUNK)
            value = jnp.dot(left, parts[:, at], preferred_element_type=jnp.float32)
            value = jnp.where(core_mask if c < CHUNKS - 1 else side_mask, value, 0.0)
            proj[:, at] = value
            square = value * value
            for t in range(CHUNK // 128):
                total = total + square[:, t * 128 : (t + 1) * 128]
        power = jnp.sum(total, axis=1, keepdims=True) * (1.0 / (EDGE * EDGE))
        return SHRINK * jnp.sqrt(power + EPSILON)

    def shrunk(level, at):
        value = proj[:, at]
        return value - jnp.clip(value, -level, level)

    def step(_, basis):
        level = project(basis)
        total = jnp.zeros((4 * RANK, 2 * frames), jnp.float32)
        for c in range(CHUNKS):
            at = pl.ds(c * CHUNK, CHUNK)
            factor = jnp.concatenate(halves(shrunk(level, at)), axis=0)
            total = total + lax.dot_general(
                factor, parts[: 2 * frames, at], NT, preferred_element_type=jnp.float32
            )
        total = total[: 2 * RANK] + total[2 * RANK :]
        total = total[:, :frames] + total[:, frames:]
        return jnp.concatenate(orthonormal_rows([total[:RANK], total[RANK:]]), axis=0)

    start = orthonormal_rows([start_ref[...]])[0]
    basis = lax.fori_loop(0, ITERS, step, jnp.concatenate([start, start], axis=0))
    basis_ref[...] = basis
    level = project(basis)
    left_half = lax.broadcasted_iota(jnp.int32, (RANK, COLS), 1) < PATCH
    for row in range(PATCH):
        factor = shrunk(level, pl.ds((row + MARGIN) * COLS, COLS))
        spatial_ref[:, row * COLS : (row + 1) * COLS] = jnp.where(
            left_half, factor[:RANK], factor[RANK:]
        )


def decompose(movie, start):
    frames = movie.shape[0]
    vmem = pl.BlockSpec(memory_space=pltpu.VMEM)
    return pl.pallas_call(
        decompose_kernel,
        out_shape=(
            jax.ShapeDtypeStruct((RANK, PATCH * COLS), jnp.float32),
            jax.ShapeDtypeStruct((2 * RANK, frames), jnp.float32),
            jax.ShapeDtypeStruct((1, PIXELS), jnp.float32),
        ),
        in_specs=[vmem, vmem],
        out_specs=(vmem, vmem, vmem),
        scratch_shapes=[
            pltpu.VMEM((4 * frames, PIXELS), jnp.bfloat16),
            pltpu.VMEM((2 * RANK, PIXELS), jnp.float32),
        ],
        compiler_params=pltpu.CompilerParams(vmem_limit_bytes=48 * 1024 * 1024),
        name="decompose",
    )(movie, start)


def place_kernel(shift_ref, frame_ref, out_ref, padded):
    height, width = frame_ref.shape
    n_cols, n_rows = out_ref.shape[:2]
    edge = SHIFT + MARGIN
    down, right = shift_ref[0], shift_ref[1]
    padded[:edge] = jnp.zeros((edge, width), jnp.float32)
    padded[edge : edge + height] = frame_ref[...]
    padded[edge + height :] = jnp.zeros((padded.shape[0] - edge - height, width), jnp.float32)
    row = lax.broadcasted_iota(jnp.int32, (EDGE, width), 0)
    col = lax.broadcasted_iota(jnp.int32, (EDGE, width), 1)
    from_col = col - right
    col_inside = (from_col >= 0) & (from_col < width)
    lane = lax.broadcasted_iota(jnp.int32, (EDGE, COLS), 1)
    row_in_tile = lax.broadcasted_iota(jnp.int32, (8, COLS), 0)
    turn = jnp.where(right < 0, right + width, right)
    ahead = SHIFT - down
    skip = ahead // 8 * 8
    lift = (EDGE + 8 - ahead % 8) % (EDGE + 8)
    nothing = jnp.zeros((EDGE, COLS), jnp.float32)
    for r in range(n_rows):
        top = r * PATCH - MARGIN
        block = padded[pl.ds(pl.multiple_of(r * PATCH + skip, 8), EDGE + 8), :]
        block = pltpu.roll(block, lift, 0)[:EDGE]
        inside = col_inside & (row + top >= 0) & (row + top < height)
        block = jnp.where(inside, pltpu.roll(block, turn, 1), 0.0)
        tiles = [block[:, c * COLS : (c + 1) * COLS] for c in range(n_cols)]
        for c in range(n_cols):
            out_ref[c, r, :EDGE, :] = tiles[c]
            left = tiles[c - 1] if c > 0 else nothing
            after = tiles[c + 1] if c + 1 < n_cols else nothing
            sides = jnp.where(lane >= COLS - MARGIN, left, jnp.where(lane < MARGIN, after, 0.0))
            group = [
                pltpu.roll(sides[8 * g : 8 * g + 8], (MARGIN + 2 * MARGIN * g) % COLS, 1)
                for g in range(EDGE // 8)
            ]
            out_ref[c, r, EDGE : EDGE + 8, :] = sum(group[1:8], group[0])
            rest = group[8] + group[9]
            spread = jnp.where(row_in_tile % 4 == 0, rest, 0.0)
            for q in range(1, 4):
                spread += jnp.where(row_in_tile % 4 == q, pltpu.roll(rest, 32 * q, 1), 0.0)
            for half in range(2):
                part = jnp.where(row_in_tile // 4 == half, spread, 0.0)
                out_ref[c, r, EDGE + 8 + half : EDGE + 9 + half, :] = jnp.sum(
                    part, axis=0, keepdims=True
                )


def place(frame, shift, n_rows, n_cols):
    height, width = frame.shape
    vmem = pl.BlockSpec(memory_space=pltpu.VMEM)
    return pl.pallas_call(
        place_kernel,
        out_shape=jax.ShapeDtypeStruct((n_cols, n_rows, PIXELS // COLS, COLS), jnp.float32),
        in_specs=[pl.BlockSpec(memory_space=pltpu.SMEM), vmem],
        out_specs=vmem,
        scratch_shapes=[pltpu.VMEM((height + 2 * (SHIFT + MARGIN) + 8, width), jnp.float32)],
        compiler_params=pltpu.CompilerParams(vmem_limit_bytes=48 * 1024 * 1024),
        name="place",
    )(shift, frame)


def on_device(frames, shifts, start_basis):
    n_rows = lax.axis_size("py")
    n_cols = lax.axis_size("px")
    assert frames.shape[1:] == (n_rows * PATCH, n_cols * COLS)
    blocks = jnp.stack(
        [place(frames[f], shifts[f], n_rows, n_cols) for f in range(frames.shape[0])]
    )
    blocks = blocks.reshape(frames.shape[0], n_rows * n_cols, PIXELS // COLS, COLS)
    arrived = lax.all_to_all(blocks, ("px", "py"), split_axis=1, concat_axis=0, tiled=True)
    arrived = arrived.reshape(-1, PIXELS // COLS, COLS)
    total_frames = arrived.shape[0]
    spatial, basis, mean = decompose(arrived, start_basis.T)
    spatial = spatial.reshape(RANK, PATCH, COLS)
    temporal = basis.reshape(1, 2, RANK, total_frames).transpose(0, 1, 3, 2) * jnp.sqrt(
        jnp.float32(total_frames)
    )
    background = mean[0, MARGIN * COLS : (MARGIN + PATCH) * COLS].reshape(PATCH, COLS)
    return (spatial, temporal, background)


def solution(mesh):
    placed = (P(("px", "py"), None, None), P(("px", "py"), None), P())
    return jax.shard_map(
        on_device,
        mesh=mesh,
        in_specs=placed,
        out_specs=(P(None, "py", "px"), P("py", "px", None, None), P("py", "px")),
        check_vma=False,
    )
```

```python
import jax
import jax.numpy as jnp
from jax import lax
from jax.experimental import pallas as pl
from jax.experimental.pallas import tpu as pltpu
from jax.sharding import PartitionSpec as P

PATCH = 64
MARGIN = 8
RANK = 16
ITERS = 6
SHIFT = 8
EDGE = PATCH + 2 * MARGIN
COLS = 2 * PATCH
CORE = EDGE * COLS
SIDE = EDGE * 2 * MARGIN
PIXELS = CORE + SIDE
CHUNK = SIDE
CHUNKS = PIXELS // CHUNK

SHRINK = 0.5
EPSILON = 1e-06
HIGH = lax.Precision.HIGHEST
NT = (((1,), (1,)), ((), ()))


def halves(value):
    high = value.astype(jnp.bfloat16)
    low = (value - high.astype(jnp.float32)).astype(jnp.bfloat16)
    return high, low


def orthonormal_rows(rows):
    rank = lax.broadcasted_iota(jnp.int32, (RANK, 1), 0)
    eye = (
        lax.broadcasted_iota(jnp.int32, (RANK, RANK), 0)
        == lax.broadcasted_iota(jnp.int32, (RANK, RANK), 1)
    )
    for sweep in range(2):
        grams = [
            lax.dot_general(z, z, NT, precision=HIGH, preferred_element_type=jnp.float32)
            + jnp.where(eye, EPSILON, 0.0)
            for z in rows
        ]
        for p in range(len(rows)):
            z, gram = rows[p], grams[p]
            columns = [jnp.broadcast_to(gram[:, m : m + 1], z.shape) for m in range(RANK)]
            pivots = jnp.zeros_like(z)
            for j in range(RANK):
                pivots = jnp.where(rank == j, columns[j], pivots)
                ratio = jnp.where(rank > j, columns[j], 0.0) * (1.0 / columns[j][j : j + 1])
                for m in range(j + 1, RANK):
                    columns[m] = columns[m] - ratio * columns[m][j : j + 1]
                z = z - ratio * z[j : j + 1]
            rows[p] = z * lax.rsqrt(pivots)
    return rows


def decompose_kernel(movie_ref, start_ref, spatial_ref, basis_ref, mean_ref, parts, proj):
    frames = movie_ref.shape[0]
    for c in range(CHUNKS):
        at = pl.ds(c * CHUNK, CHUNK)
        first_row = c * (CHUNK // COLS)
        raw = jnp.concatenate(
            [movie_ref[:, first_row + i, :] for i in range(CHUNK // COLS)], axis=1
        )
        mean = jnp.sum(raw, axis=0, keepdims=True) * (1.0 / frames)
        mean_ref[:, at] = mean
        high, low = halves(raw - mean)
        for part, value in enumerate((high, low, high, low)):
            parts[part * frames : (part + 1) * frames, at] = value

    lane = lax.broadcasted_iota(jnp.int32, (2 * RANK, CHUNK), 1)
    patch = lax.broadcasted_iota(jnp.int32, (2 * RANK, CHUNK), 0) // RANK
    from_left = lane % COLS - patch * (PATCH - MARGIN)
    core_mask = (from_left >= 0) & (from_left < PATCH + MARGIN)
    side_mask = lane % (2 * MARGIN) // MARGIN == patch

    def project(basis):
        high = basis.astype(jnp.bfloat16).astype(jnp.float32)
        low = basis - high
        left = jnp.concatenate([high, high, low, low], axis=1).astype(jnp.bfloat16)
        total = jnp.zeros((2 * RANK, 128), jnp.float32)
        for c in range(CHUNKS):
            at = pl.ds(c * CHUNK, CHUNK)
            value = jnp.dot(left, parts[:, at], preferred_element_type=jnp.float32)
            value = jnp.where(core_mask if c < CHUNKS - 1 else side_mask, value, 0.0)
            proj[:, at] = value
            square = value * value
            for t in range(CHUNK // 128):
                total = total + square[:, t * 128 : (t + 1) * 128]
        power = jnp.sum(total, axis=1, keepdims=True) * (1.0 / (EDGE * EDGE))
        return SHRINK * jnp.sqrt(power + EPSILON)

    def shrunk(level, at):
        value = proj[:, at]
        return value - jnp.clip(value, -level, level)

    def step(_, basis):
        level = project(basis)
        total = jnp.zeros((4 * RANK, 2 * frames), jnp.float32)
        for c in range(CHUNKS):
            at = pl.ds(c * CHUNK, CHUNK)
            factor = jnp.concatenate(halves(shrunk(level, at)), axis=0)
            total = total + lax.dot_general(
                factor, parts[: 2 * frames, at], NT, preferred_element_type=jnp.float32
            )
        total = total[: 2 * RANK] + total[2 * RANK :]
        total = total[:, :frames] + total[:, frames:]
        return jnp.concatenate(orthonormal_rows([total[:RANK], total[RANK:]]), axis=0)

    start = orthonormal_rows([start_ref[...]])[0]
    basis = lax.fori_loop(0, ITERS, step, jnp.concatenate([start, start], axis=0))
    basis_ref[...] = basis
    level = project(basis)
    left_half = lax.broadcasted_iota(jnp.int32, (RANK, COLS), 1) < PATCH
    for row in range(PATCH):
        factor = shrunk(level, pl.ds((row + MARGIN) * COLS, COLS))
        spatial_ref[:, row * COLS : (row + 1) * COLS] = jnp.where(
            left_half, factor[:RANK], factor[RANK:]
        )


def decompose(movie, start):
    frames = movie.shape[0]
    vmem = pl.BlockSpec(memory_space=pltpu.VMEM)
    return pl.pallas_call(
        decompose_kernel,
        out_shape=(
            jax.ShapeDtypeStruct((RANK, PATCH * COLS), jnp.float32),
            jax.ShapeDtypeStruct((2 * RANK, frames), jnp.float32),
            jax.ShapeDtypeStruct((1, PIXELS), jnp.float32),
        ),
        in_specs=[vmem, vmem],
        out_specs=(vmem, vmem, vmem),
        scratch_shapes=[
            pltpu.VMEM((4 * frames, PIXELS), jnp.bfloat16),
            pltpu.VMEM((2 * RANK, PIXELS), jnp.float32),
        ],
        compiler_params=pltpu.CompilerParams(vmem_limit_bytes=48 * 1024 * 1024),
        name="decompose",
    )(movie, start)


def place_kernel(shift_ref, frame_ref, out_ref, padded):
    height, width = frame_ref.shape
    n_cols, n_rows = out_ref.shape[:2]
    edge = SHIFT + MARGIN
    down, right = shift_ref[0], shift_ref[1]
    padded[:edge] = jnp.zeros((edge, width), jnp.float32)
    padded[edge : edge + height] = frame_ref[...]
    padded[edge + height :] = jnp.zeros((padded.shape[0] - edge - height, width), jnp.float32)
    row = lax.broadcasted_iota(jnp.int32, (EDGE, width), 0)
    col = lax.broadcasted_iota(jnp.int32, (EDGE, width), 1)
    from_col = col - right
    col_inside = (from_col >= 0) & (from_col < width)
    lane = lax.broadcasted_iota(jnp.int32, (EDGE, COLS), 1)
    row_in_tile = lax.broadcasted_iota(jnp.int32, (8, COLS), 0)
    turn = jnp.where(right < 0, right + width, right)
    ahead = SHIFT - down
    skip = ahead // 8 * 8
    lift = (EDGE + 8 - ahead % 8) % (EDGE + 8)
    nothing = jnp.zeros((EDGE, COLS), jnp.float32)
    for r in range(n_rows):
        top = r * PATCH - MARGIN
        block = padded[pl.ds(pl.multiple_of(r * PATCH + skip, 8), EDGE + 8), :]
        block = pltpu.roll(block, lift, 0)[:EDGE]
        inside = col_inside & (row + top >= 0) & (row + top < height)
        block = jnp.where(inside, pltpu.roll(block, turn, 1), 0.0)
        tiles = [block[:, c * COLS : (c + 1) * COLS] for c in range(n_cols)]
        for c in range(n_cols):
            out_ref[c, r, :EDGE, :] = tiles[c]
            left = tiles[c - 1] if c > 0 else nothing
            after = tiles[c + 1] if c + 1 < n_cols else nothing
            sides = jnp.where(lane >= COLS - MARGIN, left, jnp.where(lane < MARGIN, after, 0.0))
            group = [
                pltpu.roll(sides[8 * g : 8 * g + 8], (MARGIN + 2 * MARGIN * g) % COLS, 1)
                for g in range(EDGE // 8)
            ]
            out_ref[c, r, EDGE : EDGE + 8, :] = sum(group[1:8], group[0])
            rest = group[8] + group[9]
            spread = jnp.where(row_in_tile % 4 == 0, rest, 0.0)
            for q in range(1, 4):
                spread += jnp.where(row_in_tile % 4 == q, pltpu.roll(rest, 32 * q, 1), 0.0)
            for half in range(2):
                part = jnp.where(row_in_tile // 4 == half, spread, 0.0)
                out_ref[c, r, EDGE + 8 + half : EDGE + 9 + half, :] = jnp.sum(
                    part, axis=0, keepdims=True
                )


def place(frame, shift, n_rows, n_cols):
    height, width = frame.shape
    vmem = pl.BlockSpec(memory_space=pltpu.VMEM)
    return pl.pallas_call(
        place_kernel,
        out_shape=jax.ShapeDtypeStruct((n_cols, n_rows, PIXELS // COLS, COLS), jnp.float32),
        in_specs=[pl.BlockSpec(memory_space=pltpu.SMEM), vmem],
        out_specs=vmem,
        scratch_shapes=[pltpu.VMEM((height + 2 * (SHIFT + MARGIN) + 8, width), jnp.float32)],
        compiler_params=pltpu.CompilerParams(vmem_limit_bytes=48 * 1024 * 1024),
        name="place",
    )(shift, frame)


def on_device(frames, shifts, start_basis):
    n_rows = lax.axis_size("py")
    n_cols = lax.axis_size("px")
    assert frames.shape[1:] == (n_rows * PATCH, n_cols * COLS)
    blocks = jnp.stack(
        [place(frames[f], shifts[f], n_rows, n_cols) for f in range(frames.shape[0])]
    )
    blocks = blocks.reshape(frames.shape[0], n_rows * n_cols, PIXELS // COLS, COLS)
    arrived = lax.all_to_all(blocks, ("px", "py"), split_axis=1, concat_axis=0, tiled=True)
    arrived = arrived.reshape(-1, PIXELS // COLS, COLS)
    total_frames = arrived.shape[0]
    spatial, basis, mean = decompose(arrived, start_basis.T)
    spatial = spatial.reshape(RANK, PATCH, COLS)
    temporal = basis.reshape(1, 2, RANK, total_frames).transpose(0, 1, 3, 2) * jnp.sqrt(
        jnp.float32(total_frames)
    )
    background = mean[0, MARGIN * COLS : (MARGIN + PATCH) * COLS].reshape(PATCH, COLS)
    return (spatial, temporal, background)


def solution(mesh):
    placed = (P(("px", "py"), None, None), P(("px", "py"), None), P())
    return jax.shard_map(
        on_device,
        mesh=mesh,
        in_specs=placed,
        out_specs=(P(None, "py", "px"), P("py", "px", None, None), P("py", "px")),
        check_vma=False,
    )
```
